256 devices in a mesh: frame: 16 (over z, x_hi), row: 16 (over x_lo, y, core).
Axes of the slice: x: 4 (x_hi: 2, x_lo: 2; x = x_hi * 2 + x_lo), y: 4, z: 8, core: 2. Of those that a mesh axis runs over, the one named last changes fastest.
Arguments:
- latents: float32 [32, 64, 112, 320], P('frame', 'row'), may hold values from -8 to 8, as said below
- hint: float32 [32, 64, 112, 320], P('frame', 'row'), may hold values from -6 to 6
- norm_gains: float32 [4, 320], replicated, may hold values from 0.1 to 1.9
- norm_shifts: float32 [4, 320], replicated, may hold values from -3 to 3
- spatial_kernels: float32 [2, 3, 3, 320, 320], replicated, may hold values from -0.109375 to 0.109375
- temporal_kernels: float32 [2, 3, 320, 320], replicated, may hold values from -0.1875 to 0.1875
- zero_weight: float32 [320, 320], replicated, may hold values from -0.3125 to 0.3125
Outputs:
- block_out: float32 [32, 64, 112, 320], P('frame', 'row')
The draws below stay inside these ranges and needn't reach their ends.
Inputs may be any that keep to these rules, and one draw needn't show every extreme that they name: latents are real-valued activations of order one.
All inputs are finite; a program needn't handle non-finite values.
Results may differ from the reference program's by a relative error of at most 0.0001.
Values sent between devices are 32-bit elements; how exact they have to be, the bound alone decides.
A program may use at most 128 MiB of HBM per device.

```python
import jax
import jax.numpy as jnp
from jax import lax

C = 320
GROUPS = 32
W = 112
FRAMES = 32
ROWS = 64


def draw_latents(key, part):
    frame_pos = jnp.arange(FRAMES, dtype=jnp.float32) / (FRAMES - 1)
    row_pos = jnp.arange(ROWS, dtype=jnp.float32) / (ROWS - 1)
    scale = 0.5 + 0.5 * frame_pos[:, None, None, None] + 0.5 * row_pos[None, :, None, None]
    noise = jax.random.normal(key, (FRAMES, ROWS, W, C), jnp.float32)
    return jnp.clip(noise * scale, -8.0, 8.0)


def levels(key, extent, shards, smallest, high):
    def one(axis_at, shards_of):
        draws = jax.random.uniform(jax.random.fold_in(jax.random.fold_in(key, 6), axis_at), (shards_of,), jnp.float32, smallest / len(shards), high / len(shards))
        return jnp.repeat(jnp.exp(draws), extent[axis_at] // shards_of).reshape((-1,) + (1,) * (len(extent) - axis_at - 1))

    loudness = one(*shards[0])
    for cut in shards[1:]:
        loudness = loudness * one(*cut)
    return loudness


def bell_draw(key, shape, width, reach, shards=(), kind=jnp.bfloat16):
    loudness = levels(key, shape, shards, -0.22, 0.18) if shards else 1.0
    values = jax.random.normal(key, shape, jnp.float32) * width * loudness
    return jnp.minimum(jnp.maximum(values, -reach), reach).astype(kind)


def setup_inputs(seed: int = 0) -> dict:
    key_of = jax.random.split(jax.random.key(seed), 8)
    latents = draw_latents(jax.random.fold_in(key_of[7], 71), 0)
    hint = bell_draw(key_of[1], (FRAMES, ROWS, W, C), 1.0, 6.0, ((0, 16), (1, 16)), jnp.float32)
    norm_gains = jnp.clip(1.0 + 0.18 * jax.random.normal(key_of[2], (4, C), jnp.float32), 0.1, 1.9)
    norm_shifts = bell_draw(key_of[3], (4, C), 0.5, 3.0, (), jnp.float32)
    spatial_kernels = bell_draw(key_of[4], (2, 3, 3, C, C), (9 * C) ** -0.5, 0.109375, (), jnp.float32)
    temporal_kernels = bell_draw(key_of[5], (2, 3, C, C), (3 * C) ** -0.5, 0.1875, (), jnp.float32)
    zero_weight = bell_draw(key_of[6], (C, C), C ** -0.5, 0.3125, (), jnp.float32)
    return dict(latents=latents, hint=hint, norm_gains=norm_gains, norm_shifts=norm_shifts, spatial_kernels=spatial_kernels, temporal_kernels=temporal_kernels, zero_weight=zero_weight)


EPS = 1e-05
HIGH = lax.Precision.HIGHEST

def norm_act(value, gain, shift):
    shape = value.shape
    grouped = value.reshape(shape[:-1] + (GROUPS, shape[-1] // GROUPS))
    mean = lax.optimization_barrier(jnp.mean(grouped, axis=(0, 1, 2, 4), keepdims=True))
    variance = lax.optimization_barrier(jnp.mean(jnp.square(grouped - mean), axis=(0, 1, 2, 4), keepdims=True))
    normed = ((grouped - mean) * lax.rsqrt(variance + EPS)).reshape(shape)
    return jax.nn.silu(normed * gain + shift)

def spatial(value, kernel):
    rows = value.shape[1]
    cols = value.shape[2]
    padded = jnp.pad(value, ((0, 0), (1, 1), (1, 1), (0, 0)))
    total = jnp.zeros(value.shape, jnp.float32)
    for shift_y in range(3):
        for shift_x in range(3):
            total = total + jnp.einsum('fhwc,cd->fhwd', padded[:, shift_y:shift_y + rows, shift_x:shift_x + cols], kernel[shift_y, shift_x], precision=HIGH)
    return total

def temporal(value, kernel):
    frames = value.shape[0]
    padded = jnp.pad(value, ((1, 1), (0, 0), (0, 0), (0, 0)))
    total = jnp.zeros(value.shape, jnp.float32)
    for tap in range(3):
        total = total + jnp.einsum('fhwc,cd->fhwd', padded[tap:tap + frames], kernel[tap], precision=HIGH)
    return total

def reference(latents, hint, norm_gains, norm_shifts, spatial_kernels, temporal_kernels, zero_weight):
    control_in = latents + hint
    inner = spatial(norm_act(control_in, norm_gains[0], norm_shifts[0]), spatial_kernels[0])
    control_out = control_in + temporal(norm_act(inner, norm_gains[1], norm_shifts[1]), temporal_kernels[0])
    skip = latents + jnp.einsum('fhwc,cd->fhwd', control_out, zero_weight, precision=HIGH)
    inner = spatial(norm_act(skip, norm_gains[2], norm_shifts[2]), spatial_kernels[1])
    return skip + temporal(norm_act(inner, norm_gains[3], norm_shifts[3]), temporal_kernels[1])
```

```python
import functools

import jax
import jax.numpy as jnp
from jax import lax
from jax.experimental import pallas as pl
from jax.experimental.pallas import tpu as pltpu
from jax.sharding import PartitionSpec as P

GROUPS = 32


EPS = 1e-05
HIGH = lax.Precision.HIGHEST
MESH = pl.DeviceIdType.MESH


def extended(shard, sides, width):
    for axis, dim in sides:
        count, length = (lax.axis_size(axis), shard.shape[dim])
        up = [(i, (i + 1) % count) for i in range(count - 1)]
        down = [(j, i) for i, j in up]
        last = lax.slice_in_dim(shard, length - width, length, axis=dim)
        first = lax.slice_in_dim(shard, 0, width, axis=dim)
        before = lax.ppermute(last, axis, up)
        after = lax.ppermute(first, axis, down)
        shard = jnp.concatenate([before, shard, after], axis=dim)
    return shard


def combine_kernel(n, x_ref, o_ref, slots, send_sem, recv_sem):
    f, r = lax.axis_index("frame"), lax.axis_index("row")
    barrier = pltpu.get_barrier_semaphore()
    for d in range(1, 16):
        pl.semaphore_signal(barrier, inc=1, device_id=(f, lax.rem(r + d, 16)), device_id_type=MESH)
        pl.semaphore_signal(barrier, inc=1, device_id=(lax.rem(f + d, 16), r), device_id_type=MESH)
    pl.semaphore_wait(barrier, 30)
    tile = x_ref[...]
    for phase in range(2):
        me = r if phase == 0 else f
        s = slots.at[phase]
        s[me] = tile
        for d in range(1, 16):
            to = lax.rem(me + d, 16)
            pltpu.make_async_remote_copy(
                s.at[me],
                s.at[me],
                send_sem.at[phase],
                recv_sem.at[phase],
                device_id=(f, to) if phase == 0 else (to, r),
                device_id_type=MESH,
            ).start()
        pltpu.make_async_copy(s.at[pl.ds(0, 15)], s.at[pl.ds(0, 15)], recv_sem.at[phase]).wait()
        pltpu.make_async_copy(s.at[pl.ds(0, 15)], s.at[pl.ds(0, 15)], send_sem.at[phase]).wait()
        v = s[...]
        means = v[:, 0:1, :]
        mean = jnp.sum(means, axis=0, keepdims=True) * (1.0 / 16)
        dev = jnp.sum(v[:, 1:2, :] + (n * 16**phase) * jnp.square(means - mean), axis=0)
        at = lax.broadcasted_iota(jnp.int32, (8, 128), 0)
        tile = jnp.where(at == 0, mean[0], jnp.where(at == 1, dev, 0.0))
    o_ref[...] = tile


def combine(tile, n, cid):
    return pl.pallas_call(
        functools.partial(combine_kernel, float(n)),
        out_shape=jax.ShapeDtypeStruct((8, 128), jnp.float32),
        in_specs=[pl.BlockSpec(memory_space=pltpu.VMEM)],
        out_specs=pl.BlockSpec(memory_space=pltpu.VMEM),
        scratch_shapes=[
            pltpu.VMEM((2, 16, 8, 128), jnp.float32),
            pltpu.SemaphoreType.DMA((2,)),
            pltpu.SemaphoreType.DMA((2,)),
        ],
        compiler_params=pltpu.CompilerParams(collective_id=cid, has_side_effects=True),
    )(tile)


def group_moments(value, cid):
    width = value.shape[-1]
    positions = value.size // width
    n = positions * (width // GROUPS)
    sums = jnp.sum(value, axis=(0, 1, 2)).reshape(GROUPS, -1).sum(1)
    mean = sums / n
    centred = value - jnp.repeat(mean, width // GROUPS)
    dev = jnp.sum(centred * centred, axis=(0, 1, 2)).reshape(GROUPS, -1).sum(1)
    tile = jnp.zeros((8, 128), jnp.float32).at[0, :GROUPS].set(mean).at[1, :GROUPS].set(dev)
    tile = combine(tile, n, cid)
    return tile[0, :GROUPS], tile[1, :GROUPS] / (n * lax.axis_size("frame") * lax.axis_size("row"))


def activate(value, mean, variance, gain, shift):
    shape = value.shape
    grouped = value.reshape(shape[:-1] + (GROUPS, shape[-1] // GROUPS))
    normed = (grouped - mean[:, None]) * lax.rsqrt(variance + EPS)[:, None]
    return jax.nn.silu(normed.reshape(shape) * gain + shift)


def spatial_taps(padded_rows, kernel):
    rows = padded_rows.shape[1] - 2
    cols = padded_rows.shape[2]
    padded = jnp.pad(padded_rows, ((0, 0), (0, 0), (1, 1), (0, 0)))
    total = jnp.zeros((padded_rows.shape[0], rows, cols, kernel.shape[-1]), jnp.float32)
    for shift_y in range(3):
        for shift_x in range(3):
            total = total + jnp.einsum(
                "fhwc,cd->fhwd",
                padded[:, shift_y : shift_y + rows, shift_x : shift_x + cols],
                kernel[shift_y, shift_x],
                precision=HIGH,
            )
    return total


def temporal(value, kernel):
    frames = value.shape[0]
    padded = extended(value, (("frame", 0),), 1)
    total = jnp.zeros(value.shape, jnp.float32)
    for tap in range(3):
        total = total + jnp.einsum(
            "fhwc,cd->fhwd", padded[tap : tap + frames], kernel[tap], precision=HIGH
        )
    return total


def local(latents, hint, norm_gains, norm_shifts, spatial_kernels, temporal_kernels, zero_weight):
    control_in = latents + hint
    mean, variance = group_moments(control_in, 1)
    active = activate(control_in, mean, variance, norm_gains[0], norm_shifts[0])
    inner = spatial_taps(extended(active, (("row", 1),), 1), spatial_kernels[0])
    mean, variance = group_moments(inner, 2)
    active = activate(inner, mean, variance, norm_gains[1], norm_shifts[1])
    control_out = control_in + temporal(active, temporal_kernels[0])
    skip = latents + jnp.einsum("fhwc,cd->fhwd", control_out, zero_weight, precision=HIGH)
    mean, variance = group_moments(skip, 3)
    middle = activate(skip, mean, variance, norm_gains[2], norm_shifts[2])
    padded = extended(middle, (("row", 1),), 1)
    inner = spatial_taps(padded, spatial_kernels[1])
    mean, variance = group_moments(inner, 4)
    active = activate(inner, mean, variance, norm_gains[3], norm_shifts[3])
    return skip + temporal(active, temporal_kernels[1])


def solution(mesh):
    return jax.shard_map(
        local,
        mesh=mesh,
        in_specs=(
            P("frame", "row", None, None),
            P("frame", "row", None, None),
            P(),
            P(),
            P(),
            P(),
            P(),
        ),
        out_specs=P("frame", "row", None, None),
        check_vma=False,
    )
```

```python
import functools

import jax
import jax.numpy as jnp
from jax import lax
from jax.experimental import pallas as pl
from jax.experimental.pallas import tpu as pltpu
from jax.sharding import PartitionSpec as P

EPS = 1e-05
MESH = pl.DeviceIdType.MESH
F32, BF16 = jnp.float32, jnp.bfloat16
C = 320
W = 112
L = 128
PER = 10
K = 3 * C
ROW_LOCAL = 2 * 4 * W * PER

FARHALO, FAR, NEAR, NEARHALO = range(4)


def split(v):
    hi = v.astype(BF16)
    return hi, (v - hi.astype(F32)).astype(BF16)


def kernel(
    lat_ref, hint_ref, gain_ref, shift_ref, sk_hbm, tk_hbm, zw_hbm, out_ref,
    ci, skip, inner, act, tact, wst, wsp, wtm, wz, cols, const, slots,
    wsem, ar_s, ar_r, row_s, row_r, near_s, near_r, far_s, far_r,
):
    f, r = lax.axis_index("frame"), lax.axis_index("row")
    odd = lax.rem(f, 2)
    partner = f + 1 - 2 * odd
    outer = lax.rem(f + 15 + 2 * odd, 16)
    above, below = lax.rem(r + 15, 16), lax.rem(r + 1, 16)
    has_far = jnp.where(odd == 0, f > 0, f < 15)
    far_at, near_at = odd, 1 - odd

    barrier = pltpu.get_barrier_semaphore()
    for d in range(1, 16):
        pl.semaphore_signal(barrier, inc=1, device_id=(f, lax.rem(r + d, 16)), device_id_type=MESH)
        pl.semaphore_signal(barrier, inc=1, device_id=(lax.rem(f + d, 16), r), device_id_type=MESH)

    weight_copies = []
    for j in range(2):
        for dy in range(3):
            for dx in range(3):
                i = j * 9 + dy * 3 + dx
                weight_copies.append(pltpu.make_async_copy(sk_hbm.at[j, dy, dx], wst.at[i], wsem.at[i]))
    for j in range(2):
        for t in range(3):
            i = 18 + j * 3 + t
            tap = t + odd * (2 - 2 * t)
            weight_copies.append(pltpu.make_async_copy(tk_hbm.at[j, tap], wst.at[i], wsem.at[i]))
    weight_copies.append(pltpu.make_async_copy(zw_hbm, wst.at[24], wsem.at[24]))
    order = list(range(9)) + [18, 19, 20, 24] + list(range(9, 18)) + [21, 22, 23]
    for i in order:
        weight_copies[i].start()

    lane = lax.broadcasted_iota(jnp.int32, (C, L), 1)
    channel = lax.broadcasted_iota(jnp.int32, (C, L), 0)
    inside = lane < W
    member = jnp.where((channel >= PER * lane) & (channel < PER * lane + PER), 1.0, 0.0).astype(F32)

    def to_groups(col):
        return jnp.sum(col * member, axis=0, keepdims=True)

    def to_channels(row):
        return jnp.sum(row * member, axis=1, keepdims=True)

    def eye(dtype):
        a = lax.broadcasted_iota(jnp.int32, (C, C), 0)
        b = lax.broadcasted_iota(jnp.int32, (C, C), 1)
        return jnp.where(a == b, 1.0, 0.0).astype(dtype)

    for slot, at in ((0, far_at), (1, near_at)):
        for i in range(4):
            ci[slot, 1 + i] = jnp.zeros((C, L), F32)
            skip[slot, 1 + i] = jnp.zeros((C, L), F32)
            v = lat_ref[at, i]
            skip[slot, 1 + i, :, 0:W] = v
            ci[slot, 1 + i, :, 0:W] = v + hint_ref[at, i]

    def local_tile(read):
        total = lax.fori_loop(0, 8, lambda i, a: a + read(i // 4, lax.rem(i, 4)), jnp.zeros((C, L), F32))
        mean = to_groups(jnp.sum(total, axis=1, keepdims=True)) * (1.0 / ROW_LOCAL)
        col = to_channels(mean)

        def squares(i, a):
            c = jnp.where(inside, read(i // 4, lax.rem(i, 4)) - col, 0.0)
            return a + c * c

        dev = to_groups(jnp.sum(lax.fori_loop(0, 8, squares, jnp.zeros((C, L), F32)), axis=1, keepdims=True))
        return pack(mean, dev)

    def pack(mean, dev):
        at = lax.broadcasted_iota(jnp.int32, (8, L), 0)
        return jnp.where(at == 0, mean, jnp.where(at == 1, dev, 0.0))

    def ar_send(k, phase, tile):
        me = r if phase == 0 else f
        s = slots.at[k, phase]
        s[me] = tile
        for d in range(1, 16):
            to = lax.rem(me + d, 16)
            pltpu.make_async_remote_copy(
                s.at[me], s.at[me], ar_s.at[k, phase], ar_r.at[k, phase],
                device_id=(f, to) if phase == 0 else (to, r), device_id_type=MESH,
            ).start()

    def ar_wait(k, phase):
        s = slots.at[k, phase]
        pltpu.make_async_copy(s.at[pl.ds(0, 15)], s.at[pl.ds(0, 15)], ar_r.at[k, phase]).wait()
        v = s[...]
        means = v[:, 0:1, :]
        mean = jnp.sum(means, axis=0, keepdims=True) * (1.0 / 16)
        dev = jnp.sum(v[:, 1:2, :] + (ROW_LOCAL * 16.0**phase) * jnp.square(means - mean), axis=0)
        return mean[0], dev

    def set_const(k, mean, dev):
        rstd = lax.rsqrt(dev * (1.0 / (256.0 * ROW_LOCAL)) + EPS)
        const[0] = jnp.broadcast_to(to_channels(mean), (C, L))
        const[1] = to_channels(rstd) * cols[2 * k]
        const[2] = cols[2 * k + 1]

    def activated(v, ok):
        u = (v - const[0]) * const[1] + const[2]
        return split(jnp.where(inside & ok, u / (1.0 + jnp.exp(-u)), 0.0))

    def remote(src, dst, sends, recvs, at, device):
        return pltpu.make_async_remote_copy(
            src, dst, sends.at[at], recvs.at[at], device_id=device, device_id_type=MESH
        )

    started = []

    def edge_copies(block, buf, slot):
        return [
            remote(buf.at[slot, 4], buf.at[slot, 0], row_s, row_r, block * 6 + slot * 2, (f, below)),
            remote(buf.at[slot, 1], buf.at[slot, 5], row_s, row_r, block * 6 + slot * 2 + 1, (f, above)),
        ]

    def near_copies(block, buf):
        dev = (partner, r)
        return [
            remote(buf.at[1, 1], buf.at[2, 1], near_s, near_r, block * 3, dev),
            remote(buf.at[1, 4], buf.at[2, 4], near_s, near_r, block * 3 + 1, dev),
            remote(buf.at[1, pl.ds(2, 2)], buf.at[2, pl.ds(2, 2)], near_s, near_r, block * 3 + 2, dev),
        ]

    def far_copy(block, j):
        return remote(
            inner.at[block, FAR, pl.ds(2 * j, 2)], inner.at[block, FARHALO, pl.ds(2 * j, 2)],
            far_s, far_r, block * 2 + j, (outer, r),
        )

    def start(copies):
        for c in copies:
            c.start()
            started.append(c)

    def prep_spatial(j, dx):
        parts = []
        for dy in range(3):
            weight_copies[j * 9 + dy * 3 + dx].wait()
            hi, lo = split(wst[j * 9 + dy * 3 + dx])
            parts += [hi, hi, lo]
        t = lax.dot_general(
            eye(BF16), jnp.concatenate(parts, axis=0), (((1,), (1,)), ((), ())), preferred_element_type=F32
        )
        wsp[j, dx * C : (dx + 1) * C, :] = t.astype(BF16)

    def prep_small(dst, which):
        parts = []
        for i in which:
            weight_copies[i].wait()
            hi, lo = split(wst[i])
            parts += [hi, hi, lo]
        t = lax.dot_general(
            eye(BF16), jnp.concatenate(parts, axis=0), (((1,), (1,)), ((), ())), preferred_element_type=F32
        )
        dst[...] = t.astype(BF16)

    def act_frame(buf, slot):
        def body(i, _):
            ok = ((i > 0) | (r > 0)) & ((i < 5) | (r < 15))
            hi, lo = activated(buf[slot, i], ok)
            at = pl.ds(pl.multiple_of(i * L, L), L)
            act[slot, 0:C, at] = hi
            act[slot, C : 2 * C, at] = lo
            act[slot, 2 * C : K, at] = hi
            return 0

        lax.fori_loop(0, 6, body, 0)

    def spatial(block, slot, dst):
        def body(j, _):
            rhs = jnp.concatenate(
                [act[slot, :, pl.ds(pl.multiple_of(j * 2 * L + dy * L, L), 2 * L)] for dy in range(3)], axis=0
            )
            y = jnp.dot(wsp[block], rhs, preferred_element_type=F32)
            for h in range(2):
                part = y[:, h * L : (h + 1) * L]
                o = part[C : 2 * C] + pltpu.roll(part[0:C], 1, 1) + pltpu.roll(part[2 * C : K], L - 1, 1)
                inner[block, dst, 2 * j + h] = jnp.where(inside, o, 0.0)
            if dst == FAR:
                far_copy(block, j).start()
            return 0

        lax.fori_loop(0, 2, body, 0)

    def act_temporal(block, slot, ok):
        def body(i, _):
            hi, lo = activated(inner[block, slot, i], ok)
            at = pl.ds(pl.multiple_of(i * L, L), L)
            tact[slot, 0:C, at] = hi
            tact[slot, C : 2 * C, at] = lo
            tact[slot, 2 * C : K, at] = hi
            return 0

        lax.fori_loop(0, 4, body, 0)

    def temporal(block, own):
        def body(j, _):
            at = pl.ds(pl.multiple_of(j * 2 * L, L), 2 * L)
            rhs = jnp.concatenate([tact[own + t, :, at] for t in range(3)], axis=0)
            y = jnp.dot(wtm[block], rhs, preferred_element_type=F32)
            rows = [1 + 2 * j, 2 + 2 * j]
            if block == 0:
                co = jnp.concatenate([ci[own, rows[0]], ci[own, rows[1]]], axis=1) + y
                hi, lo = split(co)
                z = jnp.dot(wz[...], jnp.concatenate([hi, lo, hi], axis=0), preferred_element_type=F32)
                for h in range(2):
                    skip[own, rows[h]] = skip[own, rows[h]] + jnp.where(inside, z[:, h * L : (h + 1) * L], 0.0)
            else:
                for h in range(2):
                    o = skip[own, rows[h]] + y[:, h * L : (h + 1) * L]
                    out_ref[far_at if own == 0 else near_at, 2 * j + h] = o[:, 0:W]
            return 0

        lax.fori_loop(0, 2, body, 0)

    def gain_columns():
        e = eye(F32)
        for k in range(4):
            for i, src in enumerate((gain_ref, shift_ref)):
                col = jnp.sum(e * src[k : k + 1, :], axis=1, keepdims=True)
                cols[2 * k + i] = jnp.broadcast_to(col, (C, L))

    tile = local_tile(lambda a, i: ci[a, 1 + i])
    pl.semaphore_wait(barrier, 30)

    for block, buf in ((0, ci), (1, skip)):
        ar_send(2 * block, 0, tile)
        edges = [edge_copies(block, buf, slot) for slot in range(3)]
        nears = near_copies(block, buf)
        if block == 0:
            start(nears[:2])
            start(edges[1])
            start(edges[0])
            start(nears[2:])
            gain_columns()
        prep_spatial(block, 0)
        mean, dev = ar_wait(2 * block, 0)
        ar_send(2 * block, 1, pack(mean, dev))
        prep_spatial(block, 1)
        prep_spatial(block, 2)
        nears[0].wait_recv()
        nears[1].wait_recv()
        start(edges[2])
        mean, dev = ar_wait(2 * block, 1)
        set_const(2 * block, mean, dev)
        for slot, dst in ((0, FAR), (1, NEAR)):
            for c in edges[slot]:
                c.wait_recv()
            act_frame(buf, slot)
            spatial(block, slot, dst)
        tile = local_tile(lambda a, i: inner[block, FAR + a, i])
        ar_send(2 * block + 1, 0, tile)
        for c in edges[2]:
            c.wait_recv()
        nears[2].wait_recv()
        act_frame(buf, 2)
        spatial(block, 2, NEARHALO)
        mean, dev = ar_wait(2 * block + 1, 0)
        ar_send(2 * block + 1, 1, pack(mean, dev))
        prep_small(wtm.at[block], [18 + 3 * block + t for t in range(3)])
        if block == 0:
            prep_small(wz, [24])
        mean, dev = ar_wait(2 * block + 1, 1)
        set_const(2 * block + 1, mean, dev)
        for slot in (FAR, NEAR, NEARHALO):
            act_temporal(block, slot, True)
        temporal(block, 1)
        if block == 0:
            start(near_copies(1, skip)[:2])
            start(edge_copies(1, skip, 1))
            start(near_copies(1, skip)[2:])
        far_copy(block, 0).wait_recv()
        far_copy(block, 1).wait_recv()
        act_temporal(block, FARHALO, has_far)
        temporal(block, 0)
        if block == 0:
            start(edge_copies(1, skip, 0))
            tile = local_tile(lambda a, i: skip[a, 1 + i])

    for c in started:
        c.wait_send()
    for block in range(2):
        for j in range(2):
            far_copy(block, j).wait_send()
    for k in range(4):
        for phase in range(2):
            s = slots.at[k, phase]
            pltpu.make_async_copy(s.at[pl.ds(0, 15)], s.at[pl.ds(0, 15)], ar_s.at[k, phase]).wait()


def local(latents, hint, norm_gains, norm_shifts, spatial_kernels, temporal_kernels, zero_weight):
    vmem = pl.BlockSpec(memory_space=pltpu.VMEM)
    hbm = pl.BlockSpec(memory_space=pl.ANY)
    dma = pltpu.SemaphoreType.DMA
    out = pl.pallas_call(
        kernel,
        out_shape=jax.ShapeDtypeStruct((2, 4, C, W), F32),
        in_specs=[vmem] * 4 + [hbm] * 3,
        out_specs=vmem,
        scratch_shapes=[
            pltpu.VMEM((3, 6, C, L), F32),
            pltpu.VMEM((3, 6, C, L), F32),
            pltpu.VMEM((2, 4, 4, C, L), F32),
            pltpu.VMEM((3, K, 6 * L), BF16),
            pltpu.VMEM((4, K, 4 * L), BF16),
            pltpu.VMEM((25, C, C), F32),
            pltpu.VMEM((2, K, 3 * K), BF16),
            pltpu.VMEM((2, C, 3 * K), BF16),
            pltpu.VMEM((C, K), BF16),
            pltpu.VMEM((8, C, L), F32),
            pltpu.VMEM((3, C, L), F32),
            pltpu.VMEM((4, 2, 16, 8, L), F32),
            dma((25,)),
            dma((4, 2)),
            dma((4, 2)),
            dma((12,)),
            dma((12,)),
            dma((6,)),
            dma((6,)),
            dma((4,)),
            dma((4,)),
        ],
        compiler_params=pltpu.CompilerParams(
            collective_id=1, has_side_effects=True, vmem_limit_bytes=60 * 1024 * 1024
        ),
    )(
        jnp.swapaxes(latents, 2, 3), jnp.swapaxes(hint, 2, 3), norm_gains, norm_shifts,
        spatial_kernels, temporal_kernels, zero_weight,
    )
    return jnp.swapaxes(out, 2, 3)


def solution(mesh):
    return jax.shard_map(
        local,
        mesh=mesh,
        in_specs=(
            P("frame", "row", None, None),
            P("frame", "row", None, None),
            P(),
            P(),
            P(),
            P(),
            P(),
        ),
        out_specs=P("frame", "row", None, None),
        check_vma=False,
    )
```

```python
import functools

import jax
import jax.numpy as jnp
from jax import lax
from jax.experimental import pallas as pl
from jax.experimental.pallas import tpu as pltpu
from jax.sharding import PartitionSpec as P

EPS = 1e-05
MESH = pl.DeviceIdType.MESH
F32, BF16 = jnp.float32, jnp.bfloat16
C = 320
W = 112
L = 128
PER = 10
K = 3 * C
ROW_LOCAL = 2 * 4 * W * PER

FARHALO, FAR, NEAR, NEARHALO = range(4)


def split(v):
    hi = v.astype(BF16)
    return hi, (v - hi.astype(F32)).astype(BF16)


def kernel(
    lat_hbm, hint_hbm, gain_ref, shift_ref, sk_hbm, tk_hbm, zw_hbm, out_ref,
    lat_ref, hint_ref, ci, skip, inner, act, tact, wst, wsp, wtm, wz, cols, const, slots,
    in_sem, wsem, ar_s, ar_r, row_s, row_r, near_s, near_r, far_s, far_r,
):
    f, r = lax.axis_index("frame"), lax.axis_index("row")
    odd = lax.rem(f, 2)
    partner = f + 1 - 2 * odd
    outer = lax.rem(f + 15 + 2 * odd, 16)
    above, below = lax.rem(r + 15, 16), lax.rem(r + 1, 16)
    has_far = jnp.where(odd == 0, f > 0, f < 15)
    far_at, near_at = odd, 1 - odd

    barrier = pltpu.get_barrier_semaphore()
    for d in range(1, 16):
        pl.semaphore_signal(barrier, inc=1, device_id=(f, lax.rem(r + d, 16)), device_id_type=MESH)
        pl.semaphore_signal(barrier, inc=1, device_id=(lax.rem(f + d, 16), r), device_id_type=MESH)

    inputs = [
        pltpu.make_async_copy(lat_hbm, lat_ref, in_sem.at[0]),
        pltpu.make_async_copy(hint_hbm, hint_ref, in_sem.at[1]),
    ]
    for c in inputs:
        c.start()

    weight_copies = []
    for j in range(2):
        for dy in range(3):
            for dx in range(3):
                i = j * 9 + dy * 3 + dx
                weight_copies.append(pltpu.make_async_copy(sk_hbm.at[j, dy, dx], wst.at[i], wsem.at[i]))
    for j in range(2):
        for t in range(3):
            i = 18 + j * 3 + t
            tap = t + odd * (2 - 2 * t)
            weight_copies.append(pltpu.make_async_copy(tk_hbm.at[j, tap], wst.at[i], wsem.at[i]))
    weight_copies.append(pltpu.make_async_copy(zw_hbm, wst.at[24], wsem.at[24]))
    order = list(range(9)) + [18, 19, 20, 24] + list(range(9, 18)) + [21, 22, 23]
    for i in order:
        weight_copies[i].start()

    lane = lax.broadcasted_iota(jnp.int32, (C, L), 1)
    channel = lax.broadcasted_iota(jnp.int32, (C, L), 0)
    inside = lane < W
    member = jnp.where((channel >= PER * lane) & (channel < PER * lane + PER), 1.0, 0.0).astype(F32)

    def to_groups(col):
        return jnp.sum(col * member, axis=0, keepdims=True)

    def to_channels(row):
        return jnp.sum(row * member, axis=1, keepdims=True)

    def eye(dtype):
        a = lax.broadcasted_iota(jnp.int32, (C, C), 0)
        b = lax.broadcasted_iota(jnp.int32, (C, C), 1)
        return jnp.where(a == b, 1.0, 0.0).astype(dtype)

    for c in inputs:
        c.wait()

    for slot, at in ((0, far_at), (1, near_at)):
        for i in range(4):
            ci[slot, 1 + i] = jnp.zeros((C, L), F32)
            skip[slot, 1 + i] = jnp.zeros((C, L), F32)
            v = lat_ref[at, i]
            skip[slot, 1 + i, :, 0:W] = v
            ci[slot, 1 + i, :, 0:W] = v + hint_ref[at, i]

    def local_tile(read):
        total = lax.fori_loop(0, 8, lambda i, a: a + read(i // 4, lax.rem(i, 4)), jnp.zeros((C, L), F32))
        mean = to_groups(jnp.sum(total, axis=1, keepdims=True)) * (1.0 / ROW_LOCAL)
        col = to_channels(mean)

        def squares(i, a):
            c = jnp.where(inside, read(i // 4, lax.rem(i, 4)) - col, 0.0)
            return a + c * c

        dev = to_groups(jnp.sum(lax.fori_loop(0, 8, squares, jnp.zeros((C, L), F32)), axis=1, keepdims=True))
        return pack(mean, dev)

    def pack(mean, dev):
        at = lax.broadcasted_iota(jnp.int32, (8, L), 0)
        return jnp.where(at == 0, mean, jnp.where(at == 1, dev, 0.0))

    def ar_send(k, phase, tile):
        me = r if phase == 0 else f
        s = slots.at[k, phase]
        s[me] = tile
        for d in range(1, 16):
            to = lax.rem(me + d, 16)
            pltpu.make_async_remote_copy(
                s.at[me], s.at[me], ar_s.at[k, phase], ar_r.at[k, phase],
                device_id=(f, to) if phase == 0 else (to, r), device_id_type=MESH,
            ).start()

    def ar_wait(k, phase):
        s = slots.at[k, phase]
        pltpu.make_async_copy(s.at[pl.ds(0, 15)], s.at[pl.ds(0, 15)], ar_r.at[k, phase]).wait()
        v = s[...]
        means = v[:, 0:1, :]
        mean = jnp.sum(means, axis=0, keepdims=True) * (1.0 / 16)
        dev = jnp.sum(v[:, 1:2, :] + (ROW_LOCAL * 16.0**phase) * jnp.square(means - mean), axis=0)
        return mean[0], dev

    def set_const(k, mean, dev):
        rstd = lax.rsqrt(dev * (1.0 / (256.0 * ROW_LOCAL)) + EPS)
        const[0] = jnp.broadcast_to(to_channels(mean), (C, L))
        const[1] = to_channels(rstd) * cols[2 * k]
        const[2] = cols[2 * k + 1]

    def activated(v, ok):
        u = (v - const[0]) * const[1] + const[2]
        return split(jnp.where(inside & ok, u / (1.0 + jnp.exp(-u)), 0.0))

    def remote(src, dst, sends, recvs, at, device):
        return pltpu.make_async_remote_copy(
            src, dst, sends.at[at], recvs.at[at], device_id=device, device_id_type=MESH
        )

    started = []

    def edge_copies(block, buf, slot):
        return [
            remote(buf.at[slot, 4], buf.at[slot, 0], row_s, row_r, block * 6 + slot * 2, (f, below)),
            remote(buf.at[slot, 1], buf.at[slot, 5], row_s, row_r, block * 6 + slot * 2 + 1, (f, above)),
        ]

    def near_copy(block, buf, i):
        return remote(buf.at[1, 1 + i], buf.at[2, 1 + i], near_s, near_r, block * 4 + i, (partner, r))

    def far_copy(block, i):
        return remote(
            inner.at[block, FAR, i], inner.at[block, FARHALO, i], far_s, far_r, block * 4 + i, (outer, r)
        )

    def start(copies):
        for c in copies:
            c.start()
            started.append(c)

    def prep_spatial(j, dx):
        parts = []
        for dy in range(3):
            weight_copies[j * 9 + dy * 3 + dx].wait()
            hi, lo = split(wst[j * 9 + dy * 3 + dx])
            parts += [hi, hi, lo]
        t = lax.dot_general(
            eye(BF16), jnp.concatenate(parts, axis=0), (((1,), (1,)), ((), ())), preferred_element_type=F32
        )
        wsp[j, dx * C : (dx + 1) * C, :] = t.astype(BF16)

    def prep_small(dst, which):
        parts = []
        for i in which:
            weight_copies[i].wait()
            hi, lo = split(wst[i])
            parts += [hi, hi, lo]
        t = lax.dot_general(
            eye(BF16), jnp.concatenate(parts, axis=0), (((1,), (1,)), ((), ())), preferred_element_type=F32
        )
        dst[...] = t.astype(BF16)

    def act_frame(buf, slot):
        def body(i, _):
            ok = ((i > 0) | (r > 0)) & ((i < 5) | (r < 15))
            hi, lo = activated(buf[slot, i], ok)
            at = pl.ds(pl.multiple_of(i * L, L), L)
            act[slot, 0:C, at] = hi
            act[slot, C : 2 * C, at] = lo
            act[slot, 2 * C : K, at] = hi
            return 0

        lax.fori_loop(0, 6, body, 0)

    def spatial(block, slot, dst):
        def body(j, _):
            rhs = jnp.concatenate(
                [act[slot, :, pl.ds(pl.multiple_of(j * 2 * L + dy * L, L), 2 * L)] for dy in range(3)], axis=0
            )
            y = jnp.dot(wsp[block], rhs, preferred_element_type=F32)
            for h in range(2):
                part = y[:, h * L : (h + 1) * L]
                o = part[C : 2 * C] + pltpu.roll(part[0:C], 1, 1) + pltpu.roll(part[2 * C : K], L - 1, 1)
                inner[block, dst, 2 * j + h] = jnp.where(inside, o, 0.0)
            return 0

        lax.fori_loop(0, 2, body, 0)

    def act_temporal(block, slot, ok):
        def body(i, _):
            hi, lo = activated(inner[block, slot, i], ok)
            at = pl.ds(pl.multiple_of(i * L, L), L)
            tact[slot, 0:C, at] = hi
            tact[slot, C : 2 * C, at] = lo
            tact[slot, 2 * C : K, at] = hi
            return 0

        lax.fori_loop(0, 4, body, 0)

    def temporal(block, own):
        def body(j, _):
            at = pl.ds(pl.multiple_of(j * 2 * L, L), 2 * L)
            rhs = jnp.concatenate([tact[own + t, :, at] for t in range(3)], axis=0)
            y = jnp.dot(wtm[block], rhs, preferred_element_type=F32)
            rows = [1 + 2 * j, 2 + 2 * j]
            if block == 0:
                co = jnp.concatenate([ci[own, rows[0]], ci[own, rows[1]]], axis=1) + y
                hi, lo = split(co)
                z = jnp.dot(wz[...], jnp.concatenate([hi, lo, hi], axis=0), preferred_element_type=F32)
                for h in range(2):
                    skip[own, rows[h]] = skip[own, rows[h]] + jnp.where(inside, z[:, h * L : (h + 1) * L], 0.0)
            else:
                for h in range(2):
                    o = skip[own, rows[h]] + y[:, h * L : (h + 1) * L]
                    out_ref[far_at if own == 0 else near_at, 2 * j + h] = o[:, 0:W]
            return 0

        lax.fori_loop(0, 2, body, 0)

    def gain_columns():
        e = eye(F32)
        for k in range(4):
            for i, src in enumerate((gain_ref, shift_ref)):
                col = jnp.sum(e * src[k : k + 1, :], axis=1, keepdims=True)
                cols[2 * k + i] = jnp.broadcast_to(col, (C, L))

    tile = local_tile(lambda a, i: ci[a, 1 + i])
    gain_columns()
    prep_spatial(0, 0)
    pl.semaphore_wait(barrier, 30)

    for block, buf in ((0, ci), (1, skip)):
        edges = [edge_copies(block, buf, slot) for slot in range(3)]
        near = [near_copy(block, buf, i) for i in range(4)]
        far = [far_copy(block, i) for i in range(4)]
        ar_send(2 * block, 0, tile)
        if block == 0:
            start(edges[0] + edges[1])
            start(near[0:1])
            prep_spatial(block, 1)
        else:
            start(near[3:4])
            prep_spatial(block, 0)
        mean, dev = ar_wait(2 * block, 0)
        ar_send(2 * block, 1, pack(mean, dev))
        if block == 0:
            start([near[3], near[1]])
            prep_small(wz, [24])
        else:
            start(near[1:3])
            prep_spatial(block, 1)
        prep_spatial(block, 2)
        mean, dev = ar_wait(2 * block, 1)
        set_const(2 * block, mean, dev)
        if block == 0:
            start(near[2:3])
        for c in edges[0]:
            c.wait_recv()
        act_frame(buf, 0)
        spatial(block, 0, FAR)
        start(far[0:1])
        near[0].wait_recv()
        near[3].wait_recv()
        start(edges[2])
        for c in edges[1]:
            c.wait_recv()
        act_frame(buf, 1)
        spatial(block, 1, NEAR)
        tile = local_tile(lambda a, i: inner[block, FAR + a, i])
        ar_send(2 * block + 1, 0, tile)
        start(far[1:2])
        prep_small(wtm.at[block], [18 + 3 * block + t for t in range(3)])
        for c in edges[2]:
            c.wait_recv()
        near[1].wait_recv()
        near[2].wait_recv()
        act_frame(buf, 2)
        mean, dev = ar_wait(2 * block + 1, 0)
        ar_send(2 * block + 1, 1, pack(mean, dev))
        start(far[2:4])
        spatial(block, 2, NEARHALO)
        mean, dev = ar_wait(2 * block + 1, 1)
        set_const(2 * block + 1, mean, dev)
        for slot in (FAR, NEAR, NEARHALO):
            act_temporal(block, slot, True)
        temporal(block, 1)
        if block == 0:
            start([near_copy(1, skip, 0)])
            start(edge_copies(1, skip, 1))
        for c in far:
            c.wait_recv()
        act_temporal(block, FARHALO, has_far)
        temporal(block, 0)
        if block == 0:
            start(edge_copies(1, skip, 0))
            tile = local_tile(lambda a, i: skip[a, 1 + i])

    for c in started:
        c.wait_send()
    for k in range(4):
        for phase in range(2):
            s = slots.at[k, phase]
            pltpu.make_async_copy(s.at[pl.ds(0, 15)], s.at[pl.ds(0, 15)], ar_s.at[k, phase]).wait()


def local(latents, hint, norm_gains, norm_shifts, spatial_kernels, temporal_kernels, zero_weight):
    vmem = pl.BlockSpec(memory_space=pltpu.VMEM)
    hbm = pl.BlockSpec(memory_space=pl.ANY)
    dma = pltpu.SemaphoreType.DMA
    out = pl.pallas_call(
        kernel,
        out_shape=jax.ShapeDtypeStruct((2, 4, C, W), F32),
        in_specs=[hbm] * 2 + [vmem] * 2 + [hbm] * 3,
        out_specs=vmem,
        scratch_shapes=[
            pltpu.VMEM((2, 4, C, W), F32),
            pltpu.VMEM((2, 4, C, W), F32),
            pltpu.VMEM((3, 6, C, L), F32),
            pltpu.VMEM((3, 6, C, L), F32),
            pltpu.VMEM((2, 4, 4, C, L), F32),
            pltpu.VMEM((3, K, 6 * L), BF16),
            pltpu.VMEM((4, K, 4 * L), BF16),
            pltpu.VMEM((25, C, C), F32),
            pltpu.VMEM((2, K, 3 * K), BF16),
            pltpu.VMEM((2, C, 3 * K), BF16),
            pltpu.VMEM((C, K), BF16),
            pltpu.VMEM((8, C, L), F32),
            pltpu.VMEM((3, C, L), F32),
            pltpu.VMEM((4, 2, 16, 8, L), F32),
            dma((2,)),
            dma((25,)),
            dma((4, 2)),
            dma((4, 2)),
            dma((12,)),
            dma((12,)),
            dma((8,)),
            dma((8,)),
            dma((8,)),
            dma((8,)),
        ],
        compiler_params=pltpu.CompilerParams(
            collective_id=1, has_side_effects=True, vmem_limit_bytes=60 * 1024 * 1024
        ),
    )(
        jnp.swapaxes(latents, 2, 3), jnp.swapaxes(hint, 2, 3), norm_gains, norm_shifts,
        spatial_kernels, temporal_kernels, zero_weight,
    )
    return jnp.swapaxes(out, 2, 3)


def solution(mesh):
    return jax.shard_map(
        local,
        mesh=mesh,
        in_specs=(
            P("frame", "row", None, None),
            P("frame", "row", None, None),
            P(),
            P(),
            P(),
            P(),
            P(),
        ),
        out_specs=P("frame", "row", None, None),
        check_vma=False,
    )
```

```python
import functools

import jax
import jax.numpy as jnp
from jax import lax
from jax.experimental import pallas as pl
from jax.experimental.pallas import tpu as pltpu
from jax.sharding import PartitionSpec as P

EPS = 1e-05
MESH = pl.DeviceIdType.MESH
F32, BF16 = jnp.float32, jnp.bfloat16
C = 320
W = 112
L = 128
PER = 10
K = 3 * C
KEPT = 280
SPARE = C - KEPT
ROW_LOCAL = 2 * 4 * W * PER

FARHALO, FAR, NEAR, NEARHALO = range(4)


def split(v):
    hi = v.astype(BF16)
    return hi, (v - hi.astype(F32)).astype(BF16)


def packed(v):
    lane = lax.broadcasted_iota(jnp.int32, (KEPT, L), 1)
    last = v[KEPT:C]
    moved = jnp.concatenate([pltpu.roll(last, W - 16 * k, 1) for k in range(7)], axis=0)
    return jnp.concatenate([jnp.where(lane < W, v[0:KEPT], moved), last], axis=0)


def unpacked(v):
    lane = lax.broadcasted_iota(jnp.int32, (SPARE, L), 1)
    last = jnp.zeros((SPARE, L), F32)
    for k in range(7):
        moved = pltpu.roll(v[SPARE * k : SPARE * (k + 1)], 16 * k + 16, 1)
        last = jnp.where((lane >= 16 * k) & (lane < 16 * k + 16), moved, last)
    return jnp.concatenate([v, last], axis=0)


def kernel(
    lat_hbm, hint_hbm, gain_ref, shift_ref, sk_hbm, tk_hbm, zw_hbm, out_ref,
    lat_ref, hint_ref, ci, skip, inner, act, tact, wst, wsp, wtm, wz, cols, const, slots,
    in_sem, wsem, ar_s, ar_r, row_s, row_r, near_s, near_r, far_s, far_r,
):
    f, r = lax.axis_index("frame"), lax.axis_index("row")
    odd = lax.rem(f, 2)
    partner = f + 1 - 2 * odd
    outer = lax.rem(f + 15 + 2 * odd, 16)
    above, below = lax.rem(r + 15, 16), lax.rem(r + 1, 16)
    has_far = jnp.where(odd == 0, f > 0, f < 15)
    far_at, near_at = odd, 1 - odd

    barrier = pltpu.get_barrier_semaphore()
    for d in range(1, 16):
        pl.semaphore_signal(barrier, inc=1, device_id=(f, lax.rem(r + d, 16)), device_id_type=MESH)
        pl.semaphore_signal(barrier, inc=1, device_id=(lax.rem(f + d, 16), r), device_id_type=MESH)

    inputs = [
        pltpu.make_async_copy(lat_hbm, lat_ref, in_sem.at[0]),
        pltpu.make_async_copy(hint_hbm, hint_ref, in_sem.at[1]),
    ]
    for c in inputs:
        c.start()

    weight_copies = []
    for j in range(2):
        for dy in range(3):
            for dx in range(3):
                i = j * 9 + dy * 3 + dx
                weight_copies.append(pltpu.make_async_copy(sk_hbm.at[j, dy, dx], wst.at[i], wsem.at[i]))
    for j in range(2):
        for t in range(3):
            i = 18 + j * 3 + t
            tap = t + odd * (2 - 2 * t)
            weight_copies.append(pltpu.make_async_copy(tk_hbm.at[j, tap], wst.at[i], wsem.at[i]))
    weight_copies.append(pltpu.make_async_copy(zw_hbm, wst.at[24], wsem.at[24]))
    order = list(range(9)) + [18, 19, 20, 24] + list(range(9, 18)) + [21, 22, 23]
    for i in order:
        weight_copies[i].start()

    lane = lax.broadcasted_iota(jnp.int32, (C, L), 1)
    channel = lax.broadcasted_iota(jnp.int32, (C, L), 0)
    inside = lane < W
    member = jnp.where((channel >= PER * lane) & (channel < PER * lane + PER), 1.0, 0.0).astype(F32)

    def to_groups(col):
        return jnp.sum(col * member, axis=0, keepdims=True)

    def to_channels(row):
        return jnp.sum(row * member, axis=1, keepdims=True)

    def eye(dtype):
        a = lax.broadcasted_iota(jnp.int32, (C, C), 0)
        b = lax.broadcasted_iota(jnp.int32, (C, C), 1)
        return jnp.where(a == b, 1.0, 0.0).astype(dtype)

    for c in inputs:
        c.wait()

    for slot, at in ((0, far_at), (1, near_at)):
        for i in range(4):
            ci[slot, 1 + i] = jnp.zeros((C, L), F32)
            skip[slot, 1 + i] = jnp.zeros((C, L), F32)
            v = lat_ref[at, i]
            skip[slot, 1 + i, :, 0:W] = v
            ci[slot, 1 + i, :, 0:W] = v + hint_ref[at, i]
            ci[slot, 1 + i] = packed(ci[slot, 1 + i])

    def local_tile(read):
        total = lax.fori_loop(0, 8, lambda i, a: a + jnp.where(inside, read(i // 4, lax.rem(i, 4)), 0.0), jnp.zeros((C, L), F32))
        mean = to_groups(jnp.sum(total, axis=1, keepdims=True)) * (1.0 / ROW_LOCAL)
        col = to_channels(mean)

        def squares(i, a):
            c = jnp.where(inside, read(i // 4, lax.rem(i, 4)) - col, 0.0)
            return a + c * c

        dev = to_groups(jnp.sum(lax.fori_loop(0, 8, squares, jnp.zeros((C, L), F32)), axis=1, keepdims=True))
        return pack(mean, dev)

    def pack(mean, dev):
        at = lax.broadcasted_iota(jnp.int32, (8, L), 0)
        return jnp.where(at == 0, mean, jnp.where(at == 1, dev, 0.0))

    def ar_send(k, phase, tile):
        me = r if phase == 0 else f
        s = slots.at[k, phase]
        s[me] = tile
        for d in range(1, 16):
            to = lax.rem(me + d, 16)
            pltpu.make_async_remote_copy(
                s.at[me], s.at[me], ar_s.at[k, phase], ar_r.at[k, phase],
                device_id=(f, to) if phase == 0 else (to, r), device_id_type=MESH,
            ).start()

    def ar_wait(k, phase):
        s = slots.at[k, phase]
        pltpu.make_async_copy(s.at[pl.ds(0, 15)], s.at[pl.ds(0, 15)], ar_r.at[k, phase]).wait()
        v = s[...]
        means = v[:, 0:1, :]
        mean = jnp.sum(means, axis=0, keepdims=True) * (1.0 / 16)
        dev = jnp.sum(v[:, 1:2, :] + (ROW_LOCAL * 16.0**phase) * jnp.square(means - mean), axis=0)
        return mean[0], dev

    def set_const(k, mean, dev):
        rstd = lax.rsqrt(dev * (1.0 / (256.0 * ROW_LOCAL)) + EPS)
        const[0] = jnp.broadcast_to(to_channels(mean), (C, L))
        const[1] = to_channels(rstd) * cols[2 * k]
        const[2] = cols[2 * k + 1]

    def activated(v, ok):
        u = (v - const[0]) * const[1] + const[2]
        return split(jnp.where(inside & ok, u / (1.0 + jnp.exp(-u)), 0.0))

    def remote(src, dst, sends, recvs, at, device):
        return pltpu.make_async_remote_copy(
            src, dst, sends.at[at], recvs.at[at], device_id=device, device_id_type=MESH
        )

    started = []

    def sent(buf, slot, i):
        return buf.at[slot, i, pl.ds(0, KEPT)]

    def edge_copies(block, buf, slot):
        return [
            remote(sent(buf, slot, 4), sent(buf, slot, 0), row_s, row_r, block * 6 + slot * 2, (f, below)),
            remote(sent(buf, slot, 1), sent(buf, slot, 5), row_s, row_r, block * 6 + slot * 2 + 1, (f, above)),
        ]

    def near_copy(block, buf, i):
        return remote(sent(buf, 1, 1 + i), sent(buf, 2, 1 + i), near_s, near_r, block * 4 + i, (partner, r))

    def far_copy(block, i):
        own = inner.at[block]
        return remote(sent(own, FAR, i), sent(own, FARHALO, i), far_s, far_r, block * 4 + i, (outer, r))

    def start(copies):
        for c in copies:
            c.start()
            started.append(c)

    def prep_spatial(j, dx):
        parts = []
        for dy in range(3):
            weight_copies[j * 9 + dy * 3 + dx].wait()
            hi, lo = split(wst[j * 9 + dy * 3 + dx])
            parts += [hi, hi, lo]
        t = lax.dot_general(
            eye(BF16), jnp.concatenate(parts, axis=0), (((1,), (1,)), ((), ())), preferred_element_type=F32
        )
        wsp[j, dx * C : (dx + 1) * C, :] = t.astype(BF16)

    def prep_small(dst, which):
        parts = []
        for i in which:
            weight_copies[i].wait()
            hi, lo = split(wst[i])
            parts += [hi, hi, lo]
        t = lax.dot_general(
            eye(BF16), jnp.concatenate(parts, axis=0), (((1,), (1,)), ((), ())), preferred_element_type=F32
        )
        dst[...] = t.astype(BF16)

    def act_frame(buf, slot):
        def body(i, _):
            ok = ((i > 0) | (r > 0)) & ((i < 5) | (r < 15))
            hi, lo = activated(unpacked(buf[slot, i, 0:KEPT]), ok)
            at = pl.ds(pl.multiple_of(i * L, L), L)
            act[slot, 0:C, at] = hi
            act[slot, C : 2 * C, at] = lo
            act[slot, 2 * C : K, at] = hi
            return 0

        lax.fori_loop(0, 6, body, 0)

    def spatial(block, slot, dst):
        def body(j, _):
            rhs = jnp.concatenate(
                [act[slot, :, pl.ds(pl.multiple_of(j * 2 * L + dy * L, L), 2 * L)] for dy in range(3)], axis=0
            )
            y = jnp.dot(wsp[block], rhs, preferred_element_type=F32)
            for h in range(2):
                part = y[:, h * L : (h + 1) * L]
                o = part[C : 2 * C] + pltpu.roll(part[0:C], 1, 1) + pltpu.roll(part[2 * C : K], L - 1, 1)
                inner[block, dst, 2 * j + h] = packed(o) if dst == FAR else o
            return 0

        lax.fori_loop(0, 2, body, 0)

    def act_temporal(block, slot, ok):
        def body(i, _):
            v = unpacked(inner[block, slot, i, 0:KEPT]) if slot == FARHALO else inner[block, slot, i]
            hi, lo = activated(v, ok)
            at = pl.ds(pl.multiple_of(i * L, L), L)
            tact[slot, 0:C, at] = hi
            tact[slot, C : 2 * C, at] = lo
            tact[slot, 2 * C : K, at] = hi
            return 0

        lax.fori_loop(0, 4, body, 0)

    def temporal(block, own):
        def body(j, _):
            at = pl.ds(pl.multiple_of(j * 2 * L, L), 2 * L)
            rhs = jnp.concatenate([tact[own + t, :, at] for t in range(3)], axis=0)
            y = jnp.dot(wtm[block], rhs, preferred_element_type=F32)
            rows = [1 + 2 * j, 2 + 2 * j]
            if block == 0:
                co = jnp.concatenate([ci[own, rows[0]], ci[own, rows[1]]], axis=1) + y
                hi, lo = split(co)
                z = jnp.dot(wz[...], jnp.concatenate([hi, lo, hi], axis=0), preferred_element_type=F32)
                for h in range(2):
                    skip[own, rows[h]] = packed(skip[own, rows[h]] + z[:, h * L : (h + 1) * L])
            else:
                for h in range(2):
                    o = skip[own, rows[h]] + y[:, h * L : (h + 1) * L]
                    out_ref[far_at if own == 0 else near_at, 2 * j + h] = o[:, 0:W]
            return 0

        lax.fori_loop(0, 2, body, 0)

    def gain_columns():
        e = eye(F32)
        for k in range(4):
            for i, src in enumerate((gain_ref, shift_ref)):
                col = jnp.sum(e * src[k : k + 1, :], axis=1, keepdims=True)
                cols[2 * k + i] = jnp.broadcast_to(col, (C, L))

    tile = local_tile(lambda a, i: ci[a, 1 + i])
    gain_columns()
    prep_spatial(0, 0)
    pl.semaphore_wait(barrier, 30)

    for block, buf in ((0, ci), (1, skip)):
        edges = [edge_copies(block, buf, slot) for slot in range(3)]
        near = [near_copy(block, buf, i) for i in range(4)]
        far = [far_copy(block, i) for i in range(4)]
        ar_send(2 * block, 0, tile)
        if block == 0:
            start(edges[0] + edges[1])
            start(near[0:1])
            prep_spatial(block, 1)
        else:
            start(edges[0])
            start(near[3:4])
            prep_spatial(block, 0)
        mean, dev = ar_wait(2 * block, 0)
        ar_send(2 * block, 1, pack(mean, dev))
        if block == 0:
            start([near[3], near[1]])
            prep_small(wz, [24])
        else:
            start(near[1:3])
            prep_spatial(block, 1)
        prep_spatial(block, 2)
        mean, dev = ar_wait(2 * block, 1)
        set_const(2 * block, mean, dev)
        if block == 0:
            start(near[2:3])
        for c in edges[0]:
            c.wait_recv()
        act_frame(buf, 0)
        spatial(block, 0, FAR)
        start(far[0:2])
        near[0].wait_recv()
        near[3].wait_recv()
        start(edges[2])
        for c in edges[1]:
            c.wait_recv()
        act_frame(buf, 1)
        spatial(block, 1, NEAR)
        tile = local_tile(lambda a, i: inner[block, FAR + a, i])
        ar_send(2 * block + 1, 0, tile)
        start(far[2:3])
        prep_small(wtm.at[block], [18 + 3 * block + t for t in range(3)])
        for c in edges[2]:
            c.wait_recv()
        near[1].wait_recv()
        near[2].wait_recv()
        act_frame(buf, 2)
        mean, dev = ar_wait(2 * block + 1, 0)
        ar_send(2 * block + 1, 1, pack(mean, dev))
        start(far[3:4])
        spatial(block, 2, NEARHALO)
        mean, dev = ar_wait(2 * block + 1, 1)
        set_const(2 * block + 1, mean, dev)
        for slot in (FAR, NEAR, NEARHALO):
            act_temporal(block, slot, True)
        temporal(block, 1)
        if block == 0:
            start([near_copy(1, skip, 0)])
            start(edge_copies(1, skip, 1))
        for c in far:
            c.wait_recv()
        act_temporal(block, FARHALO, has_far)
        temporal(block, 0)
        if block == 0:
            tile = local_tile(lambda a, i: skip[a, 1 + i])

    for c in started:
        c.wait_send()
    for k in range(4):
        for phase in range(2):
            s = slots.at[k, phase]
            pltpu.make_async_copy(s.at[pl.ds(0, 15)], s.at[pl.ds(0, 15)], ar_s.at[k, phase]).wait()


def local(latents, hint, norm_gains, norm_shifts, spatial_kernels, temporal_kernels, zero_weight):
    vmem = pl.BlockSpec(memory_space=pltpu.VMEM)
    hbm = pl.BlockSpec(memory_space=pl.ANY)
    dma = pltpu.SemaphoreType.DMA
    out = pl.pallas_call(
        kernel,
        out_shape=jax.ShapeDtypeStruct((2, 4, C, W), F32),
        in_specs=[hbm] * 2 + [vmem] * 2 + [hbm] * 3,
        out_specs=vmem,
        scratch_shapes=[
            pltpu.VMEM((2, 4, C, W), F32),
            pltpu.VMEM((2, 4, C, W), F32),
            pltpu.VMEM((3, 6, C, L), F32),
            pltpu.VMEM((3, 6, C, L), F32),
            pltpu.VMEM((2, 4, 4, C, L), F32),
            pltpu.VMEM((3, K, 6 * L), BF16),
            pltpu.VMEM((4, K, 4 * L), BF16),
            pltpu.VMEM((25, C, C), F32),
            pltpu.VMEM((2, K, 3 * K), BF16),
            pltpu.VMEM((2, C, 3 * K), BF16),
            pltpu.VMEM((C, K), BF16),
            pltpu.VMEM((8, C, L), F32),
            pltpu.VMEM((3, C, L), F32),
            pltpu.VMEM((4, 2, 16, 8, L), F32),
            dma((2,)),
            dma((25,)),
            dma((4, 2)),
            dma((4, 2)),
            dma((12,)),
            dma((12,)),
            dma((8,)),
            dma((8,)),
            dma((8,)),
            dma((8,)),
        ],
        compiler_params=pltpu.CompilerParams(
            collective_id=1, has_side_effects=True, vmem_limit_bytes=60 * 1024 * 1024
        ),
    )(
        jnp.swapaxes(latents, 2, 3), jnp.swapaxes(hint, 2, 3), norm_gains, norm_shifts,
        spatial_kernels, temporal_kernels, zero_weight,
    )
    return jnp.swapaxes(out, 2, 3)


def solution(mesh):
    return jax.shard_map(
        local,
        mesh=mesh,
        in_specs=(
            P("frame", "row", None, None),
            P("frame", "row", None, None),
            P(),
            P(),
            P(),
            P(),
            P(),
        ),
        out_specs=P("frame", "row", None, None),
        check_vma=False,
    )
```

```python
import functools

import jax
import jax.numpy as jnp
from jax import lax
from jax.experimental import pallas as pl
from jax.experimental.pallas import tpu as pltpu
from jax.sharding import PartitionSpec as P

EPS = 1e-05
MESH = pl.DeviceIdType.MESH
F32, BF16 = jnp.float32, jnp.bfloat16
C = 320
W = 112
L = 128
PER = 10
K = 3 * C
KEPT = 280
SPARE = C - KEPT
ROW_LOCAL = 2 * 4 * W * PER

FARHALO, FAR, NEAR, NEARHALO = range(4)


def split(v):
    hi = v.astype(BF16)
    return hi, (v - hi.astype(F32)).astype(BF16)


def packed(v):
    lane = lax.broadcasted_iota(jnp.int32, (KEPT, L), 1)
    last = v[KEPT:C]
    moved = jnp.concatenate([pltpu.roll(last, W - 16 * k, 1) for k in range(7)], axis=0)
    return jnp.concatenate([jnp.where(lane < W, v[0:KEPT], moved), last], axis=0)


def unpacked(v):
    lane = lax.broadcasted_iota(jnp.int32, (SPARE, L), 1)
    last = jnp.zeros((SPARE, L), F32)
    for k in range(7):
        moved = pltpu.roll(v[SPARE * k : SPARE * (k + 1)], 16 * k + 16, 1)
        last = jnp.where((lane >= 16 * k) & (lane < 16 * k + 16), moved, last)
    return jnp.concatenate([v, last], axis=0)


def kernel(
    lat_hbm, hint_hbm, gain_ref, shift_ref, sk_hbm, tk_hbm, zw_hbm, out_ref,
    lat_ref, hint_ref, ci, skip, inner, act, tact, wst, wsp, wtm, wz, cols, const, slots,
    in_sem, wsem, ar_s, ar_r, row_s, row_r, near_s, near_r, far_s, far_r,
):
    f, r = lax.axis_index("frame"), lax.axis_index("row")
    odd = lax.rem(f, 2)
    partner = f + 1 - 2 * odd
    outer = lax.rem(f + 15 + 2 * odd, 16)
    above, below = lax.rem(r + 15, 16), lax.rem(r + 1, 16)
    has_far = jnp.where(odd == 0, f > 0, f < 15)
    far_at, near_at = odd, 1 - odd

    barrier = pltpu.get_barrier_semaphore()
    for d in range(1, 16):
        pl.semaphore_signal(barrier, inc=1, device_id=(f, lax.rem(r + d, 16)), device_id_type=MESH)
        pl.semaphore_signal(barrier, inc=1, device_id=(lax.rem(f + d, 16), r), device_id_type=MESH)

    inputs = [
        pltpu.make_async_copy(lat_hbm, lat_ref, in_sem.at[0]),
        pltpu.make_async_copy(hint_hbm, hint_ref, in_sem.at[1]),
    ]
    for c in inputs:
        c.start()

    weight_copies = []
    for j in range(2):
        for dy in range(3):
            for dx in range(3):
                i = j * 9 + dy * 3 + dx
                weight_copies.append(pltpu.make_async_copy(sk_hbm.at[j, dy, dx], wst.at[i], wsem.at[i]))
    for j in range(2):
        for t in range(3):
            i = 18 + j * 3 + t
            tap = t + odd * (2 - 2 * t)
            weight_copies.append(pltpu.make_async_copy(tk_hbm.at[j, tap], wst.at[i], wsem.at[i]))
    weight_copies.append(pltpu.make_async_copy(zw_hbm, wst.at[24], wsem.at[24]))
    order = list(range(9)) + [18, 19, 20, 24] + list(range(9, 18)) + [21, 22, 23]
    for i in order:
        weight_copies[i].start()

    lane = lax.broadcasted_iota(jnp.int32, (C, L), 1)
    channel = lax.broadcasted_iota(jnp.int32, (C, L), 0)
    inside = lane < W
    member = jnp.where((channel >= PER * lane) & (channel < PER * lane + PER), 1.0, 0.0).astype(F32)

    def to_groups(col):
        return jnp.sum(col * member, axis=0, keepdims=True)

    def to_channels(row):
        return jnp.sum(row * member, axis=1, keepdims=True)

    def eye(dtype):
        a = lax.broadcasted_iota(jnp.int32, (C, C), 0)
        b = lax.broadcasted_iota(jnp.int32, (C, C), 1)
        return jnp.where(a == b, 1.0, 0.0).astype(dtype)

    for c in inputs:
        c.wait()

    for slot, at in ((0, far_at), (1, near_at)):
        for i in range(4):
            ci[slot, 1 + i] = jnp.zeros((C, L), F32)
            skip[slot, 1 + i] = jnp.zeros((C, L), F32)
            v = lat_ref[at, i]
            skip[slot, 1 + i, :, 0:W] = v
            ci[slot, 1 + i, :, 0:W] = v + hint_ref[at, i]
            ci[slot, 1 + i] = packed(ci[slot, 1 + i])

    def local_tile(read):
        total = lax.fori_loop(0, 8, lambda i, a: a + jnp.where(inside, read(i // 4, lax.rem(i, 4)), 0.0), jnp.zeros((C, L), F32))
        mean = to_groups(jnp.sum(total, axis=1, keepdims=True)) * (1.0 / ROW_LOCAL)
        col = to_channels(mean)

        def squares(i, a):
            c = jnp.where(inside, read(i // 4, lax.rem(i, 4)) - col, 0.0)
            return a + c * c

        dev = to_groups(jnp.sum(lax.fori_loop(0, 8, squares, jnp.zeros((C, L), F32)), axis=1, keepdims=True))
        return pack(mean, dev)

    def pack(mean, dev):
        at = lax.broadcasted_iota(jnp.int32, (8, L), 0)
        return jnp.where(at == 0, mean, jnp.where(at == 1, dev, 0.0))

    def ar_send(k, phase, tile):
        me = r if phase == 0 else f
        s = slots.at[k, phase]
        s[me] = tile
        for d in range(1, 16):
            to = lax.rem(me + d, 16)
            pltpu.make_async_remote_copy(
                s.at[me], s.at[me], ar_s.at[k, phase], ar_r.at[k, phase],
                device_id=(f, to) if phase == 0 else (to, r), device_id_type=MESH,
            ).start()

    def ar_wait(k, phase):
        s = slots.at[k, phase]
        pltpu.make_async_copy(s.at[pl.ds(0, 15)], s.at[pl.ds(0, 15)], ar_r.at[k, phase]).wait()
        v = s[...]
        means = v[:, 0:1, :]
        mean = jnp.sum(means, axis=0, keepdims=True) * (1.0 / 16)
        dev = jnp.sum(v[:, 1:2, :] + (ROW_LOCAL * 16.0**phase) * jnp.square(means - mean), axis=0)
        return mean[0], dev

    def set_const(k, mean, dev):
        rstd = lax.rsqrt(dev * (1.0 / (256.0 * ROW_LOCAL)) + EPS)
        const[0] = jnp.broadcast_to(to_channels(mean), (C, L))
        const[1] = to_channels(rstd) * cols[2 * k]
        const[2] = cols[2 * k + 1]

    def activated(v, ok):
        u = (v - const[0]) * const[1] + const[2]
        return split(jnp.where(inside & ok, u / (1.0 + jnp.exp(-u)), 0.0))

    def remote(src, dst, sends, recvs, at, device):
        return pltpu.make_async_remote_copy(
            src, dst, sends.at[at], recvs.at[at], device_id=device, device_id_type=MESH
        )

    started = []

    def sent(buf, slot, i):
        return buf.at[slot, i, pl.ds(0, KEPT)]

    def edge_copies(block, buf, slot):
        return [
            remote(sent(buf, slot, 4), sent(buf, slot, 0), row_s, row_r, block * 6 + slot * 2, (f, below)),
            remote(sent(buf, slot, 1), sent(buf, slot, 5), row_s, row_r, block * 6 + slot * 2 + 1, (f, above)),
        ]

    def near_copy(block, buf, i):
        return remote(sent(buf, 1, 1 + i), sent(buf, 2, 1 + i), near_s, near_r, block * 4 + i, (partner, r))

    def far_copy(block, i):
        own = inner.at[block]
        return remote(sent(own, FAR, i), sent(own, FARHALO, i), far_s, far_r, block * 4 + i, (outer, r))

    def start(copies):
        for c in copies:
            c.start()
            started.append(c)

    def prep_spatial(j, dx):
        parts = []
        for dy in range(3):
            weight_copies[j * 9 + dy * 3 + dx].wait()
            hi, lo = split(wst[j * 9 + dy * 3 + dx])
            parts += [hi, hi, lo]
        t = lax.dot_general(
            eye(BF16), jnp.concatenate(parts, axis=0), (((1,), (1,)), ((), ())), preferred_element_type=F32
        )
        wsp[j, dx * C : (dx + 1) * C, :] = t.astype(BF16)

    def prep_small(dst, which):
        parts = []
        for i in which:
            weight_copies[i].wait()
            hi, lo = split(wst[i])
            parts += [hi, hi, lo]
        t = lax.dot_general(
            eye(BF16), jnp.concatenate(parts, axis=0), (((1,), (1,)), ((), ())), preferred_element_type=F32
        )
        dst[...] = t.astype(BF16)

    def act_frame(buf, slot):
        def body(i, _):
            ok = ((i > 0) | (r > 0)) & ((i < 5) | (r < 15))
            hi, lo = activated(unpacked(buf[slot, i, 0:KEPT]), ok)
            at = pl.ds(pl.multiple_of(i * L, L), L)
            act[slot, 0:C, at] = hi
            act[slot, C : 2 * C, at] = lo
            act[slot, 2 * C : K, at] = hi
            return 0

        lax.fori_loop(0, 6, body, 0)

    def spatial(block, slot, dst):
        def body(j, _):
            rhs = jnp.concatenate(
                [act[slot, :, pl.ds(pl.multiple_of(j * 2 * L + dy * L, L), 2 * L)] for dy in range(3)], axis=0
            )
            y = jnp.dot(wsp[block], rhs, preferred_element_type=F32)
            for h in range(2):
                part = y[:, h * L : (h + 1) * L]
                o = part[C : 2 * C] + pltpu.roll(part[0:C], 1, 1) + pltpu.roll(part[2 * C : K], L - 1, 1)
                inner[block, dst, 2 * j + h] = packed(o) if dst == FAR else o
            if dst == FAR:

                @pl.when(j == 0)
                def _():
                    far_copy(block, 0).start()
                    far_copy(block, 1).start()

            return 0

        lax.fori_loop(0, 2, body, 0)

    def act_temporal(block, slot, ok):
        def body(i, _):
            v = unpacked(inner[block, slot, i, 0:KEPT]) if slot == FARHALO else inner[block, slot, i]
            hi, lo = activated(v, ok)
            at = pl.ds(pl.multiple_of(i * L, L), L)
            tact[slot, 0:C, at] = hi
            tact[slot, C : 2 * C, at] = lo
            tact[slot, 2 * C : K, at] = hi
            return 0

        lax.fori_loop(0, 4, body, 0)

    def temporal(block, own):
        def body(j, _):
            at = pl.ds(pl.multiple_of(j * 2 * L, L), 2 * L)
            rhs = jnp.concatenate([tact[own + t, :, at] for t in range(3)], axis=0)
            y = jnp.dot(wtm[block], rhs, preferred_element_type=F32)
            rows = [1 + 2 * j, 2 + 2 * j]
            if block == 0:
                co = jnp.concatenate([ci[own, rows[0]], ci[own, rows[1]]], axis=1) + y
                hi, lo = split(co)
                z = jnp.dot(wz[...], jnp.concatenate([hi, lo, hi], axis=0), preferred_element_type=F32)
                for h in range(2):
                    skip[own, rows[h]] = packed(skip[own, rows[h]] + z[:, h * L : (h + 1) * L])
            else:
                for h in range(2):
                    o = skip[own, rows[h]] + y[:, h * L : (h + 1) * L]
                    out_ref[far_at if own == 0 else near_at, 2 * j + h] = o[:, 0:W]
            return 0

        lax.fori_loop(0, 2, body, 0)

    def gain_columns():
        e = eye(F32)
        for k in range(4):
            for i, src in enumerate((gain_ref, shift_ref)):
                col = jnp.sum(e * src[k : k + 1, :], axis=1, keepdims=True)
                cols[2 * k + i] = jnp.broadcast_to(col, (C, L))

    tile = local_tile(lambda a, i: ci[a, 1 + i])
    gain_columns()
    prep_spatial(0, 0)
    pl.semaphore_wait(barrier, 30)

    for block, buf in ((0, ci), (1, skip)):
        edges = [edge_copies(block, buf, slot) for slot in range(3)]
        near = [near_copy(block, buf, i) for i in range(4)]
        far = [far_copy(block, i) for i in range(4)]
        ar_send(2 * block, 0, tile)
        start(near[0:1])
        prep_spatial(block, 1 - block)
        mean, dev = ar_wait(2 * block, 0)
        ar_send(2 * block, 1, pack(mean, dev))
        start(edges[0])
        start(near[3:4])
        if block == 0:
            prep_small(wz, [24])
        else:
            prep_spatial(block, 1)
        prep_spatial(block, 2)
        mean, dev = ar_wait(2 * block, 1)
        start(edges[1])
        start(near[1:2])
        set_const(2 * block, mean, dev)
        for c in edges[0]:
            c.wait_recv()
        act_frame(buf, 0)
        spatial(block, 0, FAR)
        started.extend(far[0:2])
        near[0].wait_recv()
        near[3].wait_recv()
        start(edges[2])
        for c in edges[1]:
            c.wait_recv()
        act_frame(buf, 1)
        spatial(block, 1, NEAR)
        tile = local_tile(lambda a, i: inner[block, FAR + a, i])
        ar_send(2 * block + 1, 0, tile)
        start(near[2:3])
        prep_small(wtm.at[block], [18 + 3 * block + t for t in range(3)])
        mean, dev = ar_wait(2 * block + 1, 0)
        ar_send(2 * block + 1, 1, pack(mean, dev))
        start(far[2:4])
        for c in edges[2]:
            c.wait_recv()
        near[1].wait_recv()
        near[2].wait_recv()
        act_frame(buf, 2)
        spatial(block, 2, NEARHALO)
        mean, dev = ar_wait(2 * block + 1, 1)
        set_const(2 * block + 1, mean, dev)
        for slot in (FAR, NEAR, NEARHALO):
            act_temporal(block, slot, True)
        temporal(block, 1)
        for c in far:
            c.wait_recv()
        act_temporal(block, FARHALO, has_far)
        temporal(block, 0)
        if block == 0:
            tile = local_tile(lambda a, i: skip[a, 1 + i])

    for c in started:
        c.wait_send()
    for k in range(4):
        for phase in range(2):
            s = slots.at[k, phase]
            pltpu.make_async_copy(s.at[pl.ds(0, 15)], s.at[pl.ds(0, 15)], ar_s.at[k, phase]).wait()


def local(latents, hint, norm_gains, norm_shifts, spatial_kernels, temporal_kernels, zero_weight):
    vmem = pl.BlockSpec(memory_space=pltpu.VMEM)
    hbm = pl.BlockSpec(memory_space=pl.ANY)
    dma = pltpu.SemaphoreType.DMA
    out = pl.pallas_call(
        kernel,
        out_shape=jax.ShapeDtypeStruct((2, 4, C, W), F32),
        in_specs=[hbm] * 2 + [vmem] * 2 + [hbm] * 3,
        out_specs=vmem,
        scratch_shapes=[
            pltpu.VMEM((2, 4, C, W), F32),
            pltpu.VMEM((2, 4, C, W), F32),
            pltpu.VMEM((3, 6, C, L), F32),
            pltpu.VMEM((3, 6, C, L), F32),
            pltpu.VMEM((2, 4, 4, C, L), F32),
            pltpu.VMEM((3, K, 6 * L), BF16),
            pltpu.VMEM((4, K, 4 * L), BF16),
            pltpu.VMEM((25, C, C), F32),
            pltpu.VMEM((2, K, 3 * K), BF16),
            pltpu.VMEM((2, C, 3 * K), BF16),
            pltpu.VMEM((C, K), BF16),
            pltpu.VMEM((8, C, L), F32),
            pltpu.VMEM((3, C, L), F32),
            pltpu.VMEM((4, 2, 16, 8, L), F32),
            dma((2,)),
            dma((25,)),
            dma((4, 2)),
            dma((4, 2)),
            dma((12,)),
            dma((12,)),
            dma((8,)),
            dma((8,)),
            dma((8,)),
            dma((8,)),
        ],
        compiler_params=pltpu.CompilerParams(
            collective_id=1, has_side_effects=True, vmem_limit_bytes=60 * 1024 * 1024
        ),
    )(
        jnp.swapaxes(latents, 2, 3), jnp.swapaxes(hint, 2, 3), norm_gains, norm_shifts,
        spatial_kernels, temporal_kernels, zero_weight,
    )
    return jnp.swapaxes(out, 2, 3)


def solution(mesh):
    return jax.shard_map(
        local,
        mesh=mesh,
        in_specs=(
            P("frame", "row", None, None),
            P("frame", "row", None, None),
            P(),
            P(),
            P(),
            P(),
            P(),
        ),
        out_specs=P("frame", "row", None, None),
        check_vma=False,
    )
```

```python
import functools

import jax
import jax.numpy as jnp
from jax import lax
from jax.experimental import pallas as pl
from jax.experimental.pallas import tpu as pltpu
from jax.sharding import PartitionSpec as P

EPS = 1e-05
MESH = pl.DeviceIdType.MESH
F32, BF16 = jnp.float32, jnp.bfloat16
C = 320
W = 112
L = 128
PER = 10
K = 3 * C
KEPT = 280
SPARE = C - KEPT
ROW_LOCAL = 2 * 4 * W * PER

FARHALO, FAR, NEAR, NEARHALO = range(4)


def split(v):
    hi = v.astype(BF16)
    return hi, (v - hi.astype(F32)).astype(BF16)


def packed(v):
    lane = lax.broadcasted_iota(jnp.int32, (KEPT, L), 1)
    last = v[KEPT:C]
    moved = jnp.concatenate([pltpu.roll(last, W - 16 * k, 1) for k in range(7)], axis=0)
    return jnp.concatenate([jnp.where(lane < W, v[0:KEPT], moved), last], axis=0)


def unpacked(v):
    lane = lax.broadcasted_iota(jnp.int32, (SPARE, L), 1)
    last = jnp.zeros((SPARE, L), F32)
    for k in range(7):
        moved = pltpu.roll(v[SPARE * k : SPARE * (k + 1)], 16 * k + 16, 1)
        last = jnp.where((lane >= 16 * k) & (lane < 16 * k + 16), moved, last)
    return jnp.concatenate([v, last], axis=0)


def kernel(
    lat_hbm, hint_hbm, gain_ref, shift_ref, sk_hbm, tk_hbm, zw_hbm, out_ref,
    lat_ref, hint_ref, ci, skip, inner, act, tact, wst, wsp, wtm, wz, cols, const, slots,
    in_sem, wsem, ar_s, ar_r, row_s, row_r, near_s, near_r, far_s, far_r,
):
    f, r = lax.axis_index("frame"), lax.axis_index("row")
    odd = lax.rem(f, 2)
    partner = f + 1 - 2 * odd
    outer = lax.rem(f + 15 + 2 * odd, 16)
    above, below = lax.rem(r + 15, 16), lax.rem(r + 1, 16)
    has_far = jnp.where(odd == 0, f > 0, f < 15)
    far_at, near_at = odd, 1 - odd

    barrier = pltpu.get_barrier_semaphore()
    for d in range(1, 16):
        pl.semaphore_signal(barrier, inc=1, device_id=(f, lax.rem(r + d, 16)), device_id_type=MESH)
        pl.semaphore_signal(barrier, inc=1, device_id=(lax.rem(f + d, 16), r), device_id_type=MESH)

    inputs = [
        pltpu.make_async_copy(lat_hbm, lat_ref, in_sem.at[0]),
        pltpu.make_async_copy(hint_hbm, hint_ref, in_sem.at[1]),
    ]
    for c in inputs:
        c.start()

    weight_copies = []
    for j in range(2):
        for dy in range(3):
            for dx in range(3):
                i = j * 9 + dy * 3 + dx
                weight_copies.append(pltpu.make_async_copy(sk_hbm.at[j, dy, dx], wst.at[i], wsem.at[i]))
    for j in range(2):
        for t in range(3):
            i = 18 + j * 3 + t
            tap = t + odd * (2 - 2 * t)
            weight_copies.append(pltpu.make_async_copy(tk_hbm.at[j, tap], wst.at[i], wsem.at[i]))
    weight_copies.append(pltpu.make_async_copy(zw_hbm, wst.at[24], wsem.at[24]))
    order = list(range(9)) + [18, 19, 20, 24] + list(range(9, 18)) + [21, 22, 23]
    for i in order:
        weight_copies[i].start()

    lane = lax.broadcasted_iota(jnp.int32, (C, L), 1)
    channel = lax.broadcasted_iota(jnp.int32, (C, L), 0)
    inside = lane < W
    member = jnp.where((channel >= PER * lane) & (channel < PER * lane + PER), 1.0, 0.0).astype(F32)

    def to_groups(col):
        return jnp.sum(col * member, axis=0, keepdims=True)

    def to_channels(row):
        return jnp.sum(row * member, axis=1, keepdims=True)

    def eye(dtype):
        a = lax.broadcasted_iota(jnp.int32, (C, C), 0)
        b = lax.broadcasted_iota(jnp.int32, (C, C), 1)
        return jnp.where(a == b, 1.0, 0.0).astype(dtype)

    for c in inputs:
        c.wait()

    for slot, at in ((0, far_at), (1, near_at)):
        for i in range(4):
            ci[slot, 1 + i] = jnp.zeros((C, L), F32)
            skip[slot, 1 + i] = jnp.zeros((C, L), F32)
            v = lat_ref[at, i]
            skip[slot, 1 + i, :, 0:W] = v
            ci[slot, 1 + i, :, 0:W] = v + hint_ref[at, i]
            ci[slot, 1 + i] = packed(ci[slot, 1 + i])

    def local_tile(read):
        total = lax.fori_loop(0, 8, lambda i, a: a + jnp.where(inside, read(i // 4, lax.rem(i, 4)), 0.0), jnp.zeros((C, L), F32))
        mean = to_groups(jnp.sum(total, axis=1, keepdims=True)) * (1.0 / ROW_LOCAL)
        col = to_channels(mean)

        def squares(i, a):
            c = jnp.where(inside, read(i // 4, lax.rem(i, 4)) - col, 0.0)
            return a + c * c

        dev = to_groups(jnp.sum(lax.fori_loop(0, 8, squares, jnp.zeros((C, L), F32)), axis=1, keepdims=True))
        return pack(mean, dev)

    def pack(mean, dev):
        at = lax.broadcasted_iota(jnp.int32, (8, L), 0)
        return jnp.where(at == 0, mean, jnp.where(at == 1, dev, 0.0))

    def ar_send(k, phase, tile):
        me = r if phase == 0 else f
        s = slots.at[k, phase]
        s[me] = tile
        for d in range(1, 16):
            to = lax.rem(me + d, 16)
            pltpu.make_async_remote_copy(
                s.at[me], s.at[me], ar_s.at[k, phase], ar_r.at[k, phase],
                device_id=(f, to) if phase == 0 else (to, r), device_id_type=MESH,
            ).start()

    def ar_wait(k, phase):
        s = slots.at[k, phase]
        pltpu.make_async_copy(s.at[pl.ds(0, 15)], s.at[pl.ds(0, 15)], ar_r.at[k, phase]).wait()
        v = s[...]
        means = v[:, 0:1, :]
        mean = jnp.sum(means, axis=0, keepdims=True) * (1.0 / 16)
        dev = jnp.sum(v[:, 1:2, :] + (ROW_LOCAL * 16.0**phase) * jnp.square(means - mean), axis=0)
        return mean[0], dev

    def set_const(k, mean, dev):
        rstd = lax.rsqrt(dev * (1.0 / (256.0 * ROW_LOCAL)) + EPS)
        const[0] = jnp.broadcast_to(to_channels(mean), (C, L))
        const[1] = to_channels(rstd) * cols[2 * k]
        const[2] = cols[2 * k + 1]

    def activated(v, ok):
        u = (v - const[0]) * const[1] + const[2]
        return split(jnp.where(inside & ok, 0.5 * u + 0.5 * u * jnp.tanh(0.5 * u), 0.0))

    def remote(src, dst, sends, recvs, at, device):
        return pltpu.make_async_remote_copy(
            src, dst, sends.at[at], recvs.at[at], device_id=device, device_id_type=MESH
        )

    started = []

    def sent(buf, slot, i):
        return buf.at[slot, i, pl.ds(0, KEPT)]

    def edge_copies(block, buf, slot):
        return [
            remote(sent(buf, slot, 4), sent(buf, slot, 0), row_s, row_r, block * 6 + slot * 2, (f, below)),
            remote(sent(buf, slot, 1), sent(buf, slot, 5), row_s, row_r, block * 6 + slot * 2 + 1, (f, above)),
        ]

    def near_copy(block, buf, i):
        return remote(sent(buf, 1, 1 + i), sent(buf, 2, 1 + i), near_s, near_r, block * 4 + i, (partner, r))

    def far_copy(block, i):
        own = inner.at[block]
        return remote(sent(own, FAR, i), sent(own, FARHALO, i), far_s, far_r, block * 4 + i, (outer, r))

    def start(copies):
        for c in copies:
            c.start()
            started.append(c)

    def prep_spatial(j, dx):
        parts = []
        for dy in range(3):
            weight_copies[j * 9 + dy * 3 + dx].wait()
            hi, lo = split(wst[j * 9 + dy * 3 + dx])
            parts += [hi, hi, lo]
        t = lax.dot_general(
            eye(BF16), jnp.concatenate(parts, axis=0), (((1,), (1,)), ((), ())), preferred_element_type=F32
        )
        wsp[j, dx * C : (dx + 1) * C, :] = t.astype(BF16)

    def prep_small(dst, which):
        parts = []
        for i in which:
            weight_copies[i].wait()
            hi, lo = split(wst[i])
            parts += [hi, hi, lo]
        t = lax.dot_general(
            eye(BF16), jnp.concatenate(parts, axis=0), (((1,), (1,)), ((), ())), preferred_element_type=F32
        )
        dst[...] = t.astype(BF16)

    def act_frame(buf, slot):
        def body(i, _):
            ok = ((i > 0) | (r > 0)) & ((i < 5) | (r < 15))
            hi, lo = activated(unpacked(buf[slot, i, 0:KEPT]), ok)
            at = pl.ds(pl.multiple_of(i * L, L), L)
            act[slot, 0:C, at] = hi
            act[slot, C : 2 * C, at] = lo
            act[slot, 2 * C : K, at] = hi
            return 0

        lax.fori_loop(0, 6, body, 0)

    def spatial(block, slot, dst):
        def body(j, _):
            rhs = jnp.concatenate(
                [act[slot, :, pl.ds(pl.multiple_of(j * 2 * L + dy * L, L), 2 * L)] for dy in range(3)], axis=0
            )
            y = jnp.dot(wsp[block], rhs, preferred_element_type=F32)
            for h in range(2):
                part = y[:, h * L : (h + 1) * L]
                o = part[C : 2 * C] + pltpu.roll(part[0:C], 1, 1) + pltpu.roll(part[2 * C : K], L - 1, 1)
                inner[block, dst, 2 * j + h] = packed(o) if dst == FAR else o
            if dst == FAR:

                @pl.when(j == 0)
                def _():
                    far_copy(block, 0).start()
                    far_copy(block, 1).start()

            return 0

        lax.fori_loop(0, 2, body, 0)

    def act_temporal(block, slot, ok):
        def body(i, _):
            v = unpacked(inner[block, slot, i, 0:KEPT]) if slot == FARHALO else inner[block, slot, i]
            hi, lo = activated(v, ok)
            at = pl.ds(pl.multiple_of(i * L, L), L)
            tact[slot, 0:C, at] = hi
            tact[slot, C : 2 * C, at] = lo
            tact[slot, 2 * C : K, at] = hi
            return 0

        lax.fori_loop(0, 4, body, 0)

    def temporal(block, own):
        def body(j, _):
            at = pl.ds(pl.multiple_of(j * 2 * L, L), 2 * L)
            rhs = jnp.concatenate([tact[own + t, :, at] for t in range(3)], axis=0)
            y = jnp.dot(wtm[block], rhs, preferred_element_type=F32)
            rows = [1 + 2 * j, 2 + 2 * j]
            if block == 0:
                co = jnp.concatenate([ci[own, rows[0]], ci[own, rows[1]]], axis=1) + y
                hi, lo = split(co)
                z = jnp.dot(wz[...], jnp.concatenate([hi, lo, hi], axis=0), preferred_element_type=F32)
                for h in range(2):
                    skip[own, rows[h]] = packed(skip[own, rows[h]] + z[:, h * L : (h + 1) * L])
            else:
                for h in range(2):
                    o = skip[own, rows[h]] + y[:, h * L : (h + 1) * L]
                    out_ref[far_at if own == 0 else near_at, 2 * j + h] = o[:, 0:W]
            return 0

        lax.fori_loop(0, 2, body, 0)

    def gain_columns():
        e = eye(F32)
        for k in range(4):
            for i, src in enumerate((gain_ref, shift_ref)):
                col = jnp.sum(e * src[k : k + 1, :], axis=1, keepdims=True)
                cols[2 * k + i] = jnp.broadcast_to(col, (C, L))

    tile = local_tile(lambda a, i: ci[a, 1 + i])
    gain_columns()
    prep_spatial(0, 0)
    pl.semaphore_wait(barrier, 30)

    for block, buf in ((0, ci), (1, skip)):
        edges = [edge_copies(block, buf, slot) for slot in range(3)]
        near = [near_copy(block, buf, i) for i in range(4)]
        far = [far_copy(block, i) for i in range(4)]
        ar_send(2 * block, 0, tile)
        if block == 0:
            start(edges[0] + edges[1])
            start([near[0], near[3]])
            prep_spatial(block, 1)
        else:
            start(edges[0])
            start(near[3:4])
            prep_spatial(block, 0)
        mean, dev = ar_wait(2 * block, 0)
        ar_send(2 * block, 1, pack(mean, dev))
        if block == 0:
            start(near[1:3])
            prep_small(wz, [24])
        else:
            start(near[1:3])
            prep_spatial(block, 1)
        prep_spatial(block, 2)
        mean, dev = ar_wait(2 * block, 1)
        set_const(2 * block, mean, dev)
        for c in edges[0]:
            c.wait_recv()
        act_frame(buf, 0)
        spatial(block, 0, FAR)
        started.extend(far[0:2])
        near[0].wait_recv()
        near[3].wait_recv()
        start(edges[2])
        for c in edges[1]:
            c.wait_recv()
        act_frame(buf, 1)
        spatial(block, 1, NEAR)
        tile = local_tile(lambda a, i: inner[block, FAR + a, i])
        ar_send(2 * block + 1, 0, tile)
        prep_small(wtm.at[block], [18 + 3 * block + t for t in range(3)])
        for c in edges[2]:
            c.wait_recv()
        near[1].wait_recv()
        near[2].wait_recv()
        act_frame(buf, 2)
        mean, dev = ar_wait(2 * block + 1, 0)
        ar_send(2 * block + 1, 1, pack(mean, dev))
        start(far[2:4])
        spatial(block, 2, NEARHALO)
        mean, dev = ar_wait(2 * block + 1, 1)
        set_const(2 * block + 1, mean, dev)
        for slot in (FAR, NEAR, NEARHALO):
            act_temporal(block, slot, True)
        temporal(block, 1)
        if block == 0:
            start([near_copy(1, skip, 0)])
            start(edge_copies(1, skip, 1))
        for c in far:
            c.wait_recv()
        act_temporal(block, FARHALO, has_far)
        temporal(block, 0)
        if block == 0:
            tile = local_tile(lambda a, i: skip[a, 1 + i])

    for c in started:
        c.wait_send()
    for k in range(4):
        for phase in range(2):
            s = slots.at[k, phase]
            pltpu.make_async_copy(s.at[pl.ds(0, 15)], s.at[pl.ds(0, 15)], ar_s.at[k, phase]).wait()


def local(latents, hint, norm_gains, norm_shifts, spatial_kernels, temporal_kernels, zero_weight):
    vmem = pl.BlockSpec(memory_space=pltpu.VMEM)
    hbm = pl.BlockSpec(memory_space=pl.ANY)
    dma = pltpu.SemaphoreType.DMA
    out = pl.pallas_call(
        kernel,
        out_shape=jax.ShapeDtypeStruct((2, 4, C, W), F32),
        in_specs=[hbm] * 2 + [vmem] * 2 + [hbm] * 3,
        out_specs=vmem,
        scratch_shapes=[
            pltpu.VMEM((2, 4, C, W), F32),
            pltpu.VMEM((2, 4, C, W), F32),
            pltpu.VMEM((3, 6, C, L), F32),
            pltpu.VMEM((3, 6, C, L), F32),
            pltpu.VMEM((2, 4, 4, C, L), F32),
            pltpu.VMEM((3, K, 6 * L), BF16),
            pltpu.VMEM((4, K, 4 * L), BF16),
            pltpu.VMEM((25, C, C), F32),
            pltpu.VMEM((2, K, 3 * K), BF16),
            pltpu.VMEM((2, C, 3 * K), BF16),
            pltpu.VMEM((C, K), BF16),
            pltpu.VMEM((8, C, L), F32),
            pltpu.VMEM((3, C, L), F32),
            pltpu.VMEM((4, 2, 16, 8, L), F32),
            dma((2,)),
            dma((25,)),
            dma((4, 2)),
            dma((4, 2)),
            dma((12,)),
            dma((12,)),
            dma((8,)),
            dma((8,)),
            dma((8,)),
            dma((8,)),
        ],
        compiler_params=pltpu.CompilerParams(
            collective_id=1, has_side_effects=True, vmem_limit_bytes=60 * 1024 * 1024
        ),
    )(
        jnp.swapaxes(latents, 2, 3), jnp.swapaxes(hint, 2, 3), norm_gains, norm_shifts,
        spatial_kernels, temporal_kernels, zero_weight,
    )
    return jnp.swapaxes(out, 2, 3)


def solution(mesh):
    return jax.shard_map(
        local,
        mesh=mesh,
        in_specs=(
            P("frame", "row", None, None),
            P("frame", "row", None, None),
            P(),
            P(),
            P(),
            P(),
            P(),
        ),
        out_specs=P("frame", "row", None, None),
        check_vma=False,
    )
```
